256 devices in a mesh: dp: 16 (over z_lo, y), expert: 16 (over z_hi, x, core).
Axes of the slice: x: 4, y: 4, z: 8 (z_hi: 2, z_lo: 4; z = z_hi * 4 + z_lo), core: 2. Of those that a mesh axis runs over, the one named last changes fastest.
Arguments:
- tokens: float32 [256, 256, 1280], P(('dp', 'expert')), may hold values from -8 to 8
- router: float32 [1280, 16], replicated, may hold values from -1 to 1
- w_in: float32 [16, 1280, 5120], P('expert', None, 'dp'), may hold values from -0.15625 to 0.15625
- w_out: float32 [16, 5120, 1280], P('expert', 'dp'), may hold values from -0.078125 to 0.078125
- cotangent: float32 [256, 256, 1280], P(('dp', 'expert')), may hold values from -6 to 6
Outputs:
- grad_tokens: float32 [256, 256, 1280], P(('dp', 'expert'))
- grad_router: float32 [1280, 16], replicated
- grad_w_in: float32 [16, 1280, 5120], P('expert', None, 'dp')
- grad_w_out: float32 [16, 5120, 1280], P('expert', 'dp')
The draws below stay inside these ranges and needn't reach their ends.
All inputs are finite; a program needn't handle non-finite values.
Results may differ from the reference program's by a relative error of at most 0.00021.
Values sent between devices are 32-bit elements; how exact they have to be, the bound alone decides.
No kernel may reach another device: no remote copies, remote signals or barrier semaphores. Data moves between devices by JAX's collectives and lax.ppermute only.
A program may use at most 64 MiB of HBM per device.

```python
import jax
import jax.numpy as jnp
from jax import lax

D = 1280
HID = 5120
P_SIZE = 256
EXPERTS = 16
IMAGES = 256


def draw_tokens(key, part):
    own_key = jax.random.fold_in(key, 3)
    return jax.random.truncated_normal(own_key, -6.0, 6.0, (IMAGES, P_SIZE, D), jnp.float32)


def draw_router(key, part):
    own_key = jax.random.fold_in(key, 5)
    return jax.random.truncated_normal(own_key, -4.0, 4.0, (D, EXPERTS), jnp.float32) / jnp.sqrt(jnp.float32(D))


def block_levels(stream_key, shape, shards, smallest, high):
    factor_of, own = 1.0, jax.random.fold_in(stream_key, 6)
    for axis_at, shards_of in shards:
        steps = jnp.exp(jax.random.uniform(jax.random.fold_in(own, axis_at), (shards_of,), jnp.float32, smallest / len(shards), high / len(shards)))
        factor_of = factor_of * jnp.repeat(steps, shape[axis_at] // shards_of).reshape([-1 if axis == axis_at else 1 for axis in range(len(shape))])
    return factor_of


def scatter_about(stream_key, extent, spread, most, cuts=(), kind=jnp.bfloat16):
    entries = jax.random.normal(stream_key, extent, jnp.float32) * spread
    if len(cuts) > 0:
        entries = block_levels(stream_key, extent, cuts, -0.22, 0.18) * entries
    return jnp.clip(entries, min=-most, max=most).astype(kind)


def setup_inputs(seed: int = 0) -> dict:
    splits = jax.random.split(jax.random.key(seed), 6)
    return {
        "tokens": draw_tokens(jax.random.fold_in(splits[5], 71), 0),
        "router": draw_router(jax.random.fold_in(splits[5], 71), 0),
        "w_in": scatter_about(splits[2], (EXPERTS, D, HID), D ** -0.5, 0.15625, ((0, 16), (2, 16)), jnp.float32),
        "w_out": scatter_about(splits[3], (EXPERTS, HID, D), HID ** -0.5, 0.078125, ((0, 16), (1, 16)), jnp.float32),
        "cotangent": scatter_about(splits[4], (IMAGES, P_SIZE, D), 1.0, 6.0, ((0, 256),), jnp.float32),
    }


highest = lax.Precision.HIGHEST

def forward(tokens, router, w_in, w_out):
    logits = jnp.einsum('ipd,de->ipe', tokens, router, precision=highest)
    dispatch = jax.nn.softmax(logits, axis=1)
    combine = jax.nn.softmax(logits, axis=2)
    slot_in = jnp.einsum('ipe,ipd->ied', dispatch, tokens, precision=highest)
    pre_act = jnp.einsum('ied,edh->ieh', slot_in, w_in, precision=highest)
    hidden = jax.nn.gelu(pre_act)
    slot_out = jnp.einsum('ieh,ehd->ied', hidden, w_out, precision=highest)
    return jnp.einsum('ipe,ied->ipd', combine, slot_out, precision=highest)

def reference(tokens, router, w_in, w_out, cotangent):
    output, pullback = jax.vjp(forward, tokens, router, w_in, w_out)
    grad_tokens, grad_router, grad_w_in, grad_w_out = pullback(cotangent)
    return (grad_tokens, grad_router, grad_w_in, grad_w_out)
```

```python
import jax
import jax.numpy as jnp
from jax import lax
from jax.sharding import Mesh, PartitionSpec as P

highest = lax.Precision.HIGHEST
high = lax.Precision.HIGH

DP = ("zl", "y")
EX = ("zh", "x", "c")
ZEX = ("zl",) + EX
ALL = DP + EX
UP = [(i, (i + 1) % 4) for i in range(4)]
DOWN = [(i, (i - 1) % 4) for i in range(4)]


def gather_y(block):
    half = block.shape[0] // 2
    from_below = lax.ppermute(block, "y", UP)
    from_above = lax.ppermute(block, "y", DOWN)
    far_a = lax.ppermute(from_below[:half], "y", UP)
    far_b = lax.ppermute(from_above[half:], "y", DOWN)
    return jnp.concatenate([block, from_below, from_above, far_a, far_b])


def scatter_y(parts):
    n = parts.shape[0] // 4
    half = n // 2
    own, below, above = parts[:n], parts[n : 2 * n], parts[2 * n : 3 * n]
    far_a, far_b = parts[3 * n : 3 * n + half], parts[3 * n + half :]
    got_a = lax.ppermute(far_a, "y", DOWN)
    got_b = lax.ppermute(far_b, "y", UP)
    to_below = jnp.concatenate([below[:half] + got_a, below[half:]])
    to_above = jnp.concatenate([above[:half], above[half:] + got_b])
    return own + lax.ppermute(to_below, "y", DOWN) + lax.ppermute(to_above, "y", UP)


def sum_all(local):
    e, d = local.shape
    lanes = 128
    n = e * d // lanes
    pieces = jnp.pad(local.reshape(n, 1, lanes), ((0, 256 - n), (0, 0), (0, 0)))
    mine = lax.all_to_all(pieces, ALL, 0, 0, tiled=True)
    total = jnp.sum(mine, axis=0, keepdims=True)
    back = lax.all_to_all(jnp.broadcast_to(total, (256, 1, lanes)), ALL, 0, 0, tiled=True)
    return back[:n].reshape(e, d)


def on_device(tokens, router, w_in, w_out, cotangent):
    tokens, cotangent = tokens[0], cotangent[0]
    w_in, w_out = w_in[0], w_out[0]
    width = tokens.shape[1]
    n_exp = router.shape[1]
    logits = jnp.einsum("pd,de->pe", tokens, router, precision=highest)
    dispatch = jax.nn.softmax(logits, axis=0)
    combine = jax.nn.softmax(logits, axis=1)
    slot_in = jnp.einsum("pe,pd->ed", dispatch, tokens, precision=high)
    d_slot_out = jnp.einsum("pe,pd->ed", combine, cotangent, precision=high)
    both = jnp.concatenate([slot_in, d_slot_out], axis=1)
    sent = jnp.broadcast_to(both[None], (4, n_exp, 2 * width)).reshape(4 * n_exp, 2 * width)
    arrived = lax.all_to_all(sent, ZEX, 0, 0, tiled=True)
    gathered = gather_y(arrived)
    x, dy = gathered[:, :width], gathered[:, width:]
    pre_act = jnp.einsum("rd,dh->rh", x, w_in, precision=high)
    hidden, gelu_pull = jax.vjp(jax.nn.gelu, pre_act)
    d_hidden = jnp.einsum("rd,hd->rh", dy, w_out, precision=high)
    d_pre = gelu_pull(d_hidden)[0]
    part_out = jnp.einsum("rh,hd->rd", hidden, w_out, precision=high)
    part_grad = jnp.einsum("rh,dh->rd", d_pre, w_in, precision=high)
    summed = scatter_y(jnp.concatenate([part_out, part_grad], axis=1))
    grad_w_out = jnp.einsum("rh,rd->hd", hidden, dy, precision=high)
    grad_w_in = jnp.einsum("rd,rh->dh", x, d_pre, precision=high)
    back = lax.all_to_all(summed, ZEX, 0, 0, tiled=True)
    back = jnp.sum(back.reshape(4, n_exp, 2 * width), axis=0)
    slot_out, d_slot_in = back[:, :width], back[:, width:]
    d_comb = jnp.einsum("pd,ed->pe", cotangent, slot_out, precision=high)
    d_disp = jnp.einsum("pd,ed->pe", tokens, d_slot_in, precision=high)
    d_logits = dispatch * (d_disp - jnp.sum(dispatch * d_disp, axis=0, keepdims=True))
    d_logits = d_logits + combine * (d_comb - jnp.sum(combine * d_comb, axis=1, keepdims=True))
    local_router = jnp.einsum("pe,pd->ed", d_logits, tokens, precision=high)
    grad_router = sum_all(local_router).T
    grad_tokens = jnp.einsum("pe,ed->pd", dispatch, d_slot_in, precision=high)
    grad_tokens = grad_tokens + jnp.einsum("pe,de->pd", d_logits, router, precision=high)
    return (grad_tokens[None], grad_router, grad_w_in[None], grad_w_out[None])


def solution(mesh):
    split = Mesh(mesh.devices.reshape(4, 4, 2, 4, 2), ALL)
    return jax.shard_map(
        on_device,
        mesh=split,
        in_specs=(
            P(ALL, None, None),
            P(),
            P(EX, None, DP),
            P(EX, DP, None),
            P(ALL, None, None),
        ),
        out_specs=(
            P(ALL, None, None),
            P(),
            P(EX, None, DP),
            P(EX, DP, None),
        ),
        check_vma=False,
    )
```

```python
import jax
import jax.numpy as jnp
from jax import lax
from jax.sharding import Mesh, PartitionSpec as P

highest = lax.Precision.HIGHEST
high = lax.Precision.HIGH

DP = ("zl", "y")
EX = ("zh", "x", "c")
ZEX = ("zl",) + EX
ALL = DP + EX
UP = [(i, (i + 1) % 4) for i in range(4)]
DOWN = [(i, (i - 1) % 4) for i in range(4)]


def gather_y(block):
    half = block.shape[0] // 2
    from_below = lax.ppermute(block, "y", UP)
    from_above = lax.ppermute(block, "y", DOWN)
    far_a = lax.ppermute(from_below[:half], "y", UP)
    far_b = lax.ppermute(from_above[half:], "y", DOWN)
    return jnp.concatenate([block, from_below, from_above, far_a, far_b])


def scatter_y(parts):
    n = parts.shape[0] // 4
    half = n // 2
    own, below, above = parts[:n], parts[n : 2 * n], parts[2 * n : 3 * n]
    far_a, far_b = parts[3 * n : 3 * n + half], parts[3 * n + half :]
    got_a = lax.ppermute(far_a, "y", DOWN)
    got_b = lax.ppermute(far_b, "y", UP)
    to_below = jnp.concatenate([below[:half] + got_a, below[half:]])
    to_above = jnp.concatenate([above[:half], above[half:] + got_b])
    return own + lax.ppermute(to_below, "y", DOWN) + lax.ppermute(to_above, "y", UP)


def sum_axis(block, axis):
    total = block
    for k in range(1, 4):
        total = total + lax.ppermute(block, axis, [(i, (i + k) % 4) for i in range(4)])
    return total


def sum_all(local):
    swap = [(0, 1), (1, 0)]
    first = lax.axis_index("c") == 0
    half = local.shape[0] // 2
    low, top = local[:half], local[half:]
    mine = jnp.where(first, low, top) + lax.ppermute(jnp.where(first, top, low), "c", swap)
    mine = sum_axis(sum_axis(mine, "x"), "y")
    pieces = jnp.broadcast_to(mine[None], (8,) + mine.shape)
    mine = jnp.sum(lax.all_to_all(pieces, ("zl", "zh"), 0, 0, tiled=True), axis=0)
    other = lax.ppermute(mine, "c", swap)
    return jnp.where(first, jnp.concatenate([mine, other]), jnp.concatenate([other, mine]))


def on_device(tokens, router, w_in, w_out, cotangent):
    tokens, cotangent = tokens[0], cotangent[0]
    w_in, w_out = w_in[0], w_out[0]
    width = tokens.shape[1]
    n_exp = router.shape[1]
    logits = jnp.einsum("pd,de->pe", tokens, router, precision=highest)
    dispatch = jax.nn.softmax(logits, axis=0)
    combine = jax.nn.softmax(logits, axis=1)
    slot_in = jnp.einsum("pe,pd->ed", dispatch, tokens, precision=high)
    d_slot_out = jnp.einsum("pe,pd->ed", combine, cotangent, precision=high)
    both = jnp.concatenate([slot_in, d_slot_out], axis=1)
    sent = jnp.broadcast_to(both[None], (4, n_exp, 2 * width)).reshape(4 * n_exp, 2 * width)
    arrived = lax.all_to_all(sent, ZEX, 0, 0, tiled=True)
    x = gather_y(arrived[:, :width])
    dy = gather_y(arrived[:, width:])
    pre_act = jnp.einsum("rd,dh->rh", x, w_in, precision=high)
    hidden, gelu_pull = jax.vjp(jax.nn.gelu, pre_act)
    d_hidden = jnp.einsum("rd,hd->rh", dy, w_out, precision=high)
    d_pre = gelu_pull(d_hidden)[0]
    part_out = jnp.einsum("rh,hd->rd", hidden, w_out, precision=high)
    part_grad = jnp.einsum("rh,dh->rd", d_pre, w_in, precision=high)
    summed = jnp.concatenate([scatter_y(part_out), scatter_y(part_grad)], axis=1)
    grad_w_out = jnp.einsum("rh,rd->hd", hidden, dy, precision=high)
    grad_w_in = jnp.einsum("rd,rh->dh", x, d_pre, precision=high)
    back = lax.all_to_all(summed, ZEX, 0, 0, tiled=True)
    back = jnp.sum(back.reshape(4, n_exp, 2 * width), axis=0)
    slot_out, d_slot_in = back[:, :width], back[:, width:]
    d_comb = jnp.einsum("pd,ed->pe", cotangent, slot_out, precision=high)
    d_disp = jnp.einsum("pd,ed->pe", tokens, d_slot_in, precision=high)
    d_logits = dispatch * (d_disp - jnp.sum(dispatch * d_disp, axis=0, keepdims=True))
    d_logits = d_logits + combine * (d_comb - jnp.sum(combine * d_comb, axis=1, keepdims=True))
    local_router = jnp.einsum("pe,pd->ed", d_logits, tokens, precision=high)
    grad_router = sum_all(local_router).T
    grad_tokens = jnp.einsum("pe,ed->pd", dispatch, d_slot_in, precision=high)
    grad_tokens = grad_tokens + jnp.einsum("pe,de->pd", d_logits, router, precision=high)
    return (grad_tokens[None], grad_router, grad_w_in[None], grad_w_out[None])


def solution(mesh):
    split = Mesh(mesh.devices.reshape(4, 4, 2, 4, 2), ALL)
    return jax.shard_map(
        on_device,
        mesh=split,
        in_specs=(
            P(ALL, None, None),
            P(),
            P(EX, None, DP),
            P(EX, DP, None),
            P(ALL, None, None),
        ),
        out_specs=(
            P(ALL, None, None),
            P(),
            P(EX, None, DP),
            P(EX, DP, None),
        ),
        check_vma=False,
    )
```

```python
import jax
import jax.numpy as jnp
from jax import lax
from jax.experimental import pallas as pl
from jax.experimental.pallas import tpu as pltpu
from jax.sharding import Mesh, PartitionSpec as P

highest = lax.Precision.HIGHEST
high = lax.Precision.HIGH

DP = ("zl", "y")
EX = ("zh", "x", "c")
ZEX = ("zl",) + EX
ALL = DP + EX
UP = [(i, (i + 1) % 4) for i in range(4)]
DOWN = [(i, (i - 1) % 4) for i in range(4)]


def gather_y(block):
    half = block.shape[0] // 2
    from_below = lax.ppermute(block, "y", UP)
    from_above = lax.ppermute(block, "y", DOWN)
    far_a = lax.ppermute(from_below[:half], "y", UP)
    far_b = lax.ppermute(from_above[half:], "y", DOWN)
    return jnp.concatenate([block, from_below, from_above, far_a, far_b])


def scatter_y(parts):
    n = parts.shape[0] // 4
    half = n // 2
    own, below, above, far = parts[:n], parts[n : 2 * n], parts[2 * n : 3 * n], parts[3 * n :]
    down = lax.ppermute(jnp.concatenate([below[half:], far[:half]]), "y", DOWN)
    up = lax.ppermute(jnp.concatenate([above[:half], far[half:]]), "y", UP)
    down, up = lax.optimization_barrier((down, up))
    low, top = lax.optimization_barrier((below[:half] + down[half:], above[half:] + up[half:]))
    low, top = lax.ppermute(low, "y", DOWN), lax.ppermute(top, "y", UP)
    low, top = lax.optimization_barrier((low, top))
    return jnp.concatenate([own[:half] + up[:half] + low, own[half:] + down[:half] + top])


def sum_axis(block, axis):
    total = block
    for k in range(1, 4):
        total = total + lax.ppermute(block, axis, [(i, (i + k) % 4) for i in range(4)])
    return total


def sum_all(local, beside):
    swap = [(0, 1), (1, 0)]
    first = lax.axis_index("c") == 0
    half = local.shape[0] // 2
    low, top = local[:half], local[half:]
    mine = jnp.where(first, low, top) + lax.ppermute(jnp.where(first, top, low), "c", swap)
    mine = sum_axis(sum_axis(mine, "x"), "y")
    pieces = jnp.broadcast_to(mine[None], (8,) + mine.shape)
    mine = jnp.sum(lax.all_to_all(pieces, ("zl", "zh"), 0, 0, tiled=True), axis=0)
    mine, beside = lax.optimization_barrier((mine, beside))
    other = lax.ppermute(mine, "c", swap)
    return jnp.where(first, jnp.concatenate([mine, other]), jnp.concatenate([other, mine])), beside


def split(a):
    top = a.astype(jnp.bfloat16)
    return top, (a - top.astype(jnp.float32)).astype(jnp.bfloat16)


def dot3(a, b, dims):
    (a_top, a_low), (b_top, b_low) = a, b
    dot = lambda u, v: lax.dot_general(u, v, (dims, ((), ())), preferred_element_type=jnp.float32)
    return dot(a_low, b_top) + dot(a_top, b_low) + dot(a_top, b_top)


PIECES = 4


def fetch(source, target, sems):
    rows = target.shape[0] // PIECES
    return [
        pltpu.make_async_copy(
            source.at[pl.ds(k * rows, rows)], target.at[pl.ds(k * rows, rows)], sems.at[k]
        )
        for k in range(PIECES)
    ]


def route_kernel(
    tokens_hbm, cotangent_hbm, router_ref, sent_ref, dispatch_ref, combine_ref, tokens_ref, cotangent_ref, sems
):
    e, d = router_ref.shape
    first = fetch(tokens_hbm, tokens_ref, sems.at[0])
    second = fetch(cotangent_hbm, cotangent_ref, sems.at[1])
    for copy in first + second:
        copy.start()
    half = tokens_ref.shape[0] // 2
    parts = []
    for k in range(2):
        for copy in first[k * PIECES // 2 : (k + 1) * PIECES // 2]:
            copy.wait()
        parts.append(
            lax.dot_general(
                router_ref[...],
                tokens_ref[k * half : (k + 1) * half, :],
                (((1,), (1,)), ((), ())),
                precision=highest,
                preferred_element_type=jnp.float32,
            )
        )
    logits = jnp.concatenate(parts, axis=1)
    tokens = tokens_ref[...]
    by_token = jnp.exp(logits - jnp.max(logits, axis=1, keepdims=True))
    dispatch = by_token / jnp.sum(by_token, axis=1, keepdims=True)
    by_expert = jnp.exp(logits - jnp.max(logits, axis=0, keepdims=True))
    combine = by_expert / jnp.sum(by_expert, axis=0, keepdims=True)
    dispatch_ref[...] = dispatch
    combine_ref[...] = combine
    slot_in = dot3(split(dispatch), split(tokens), ((1,), (0,)))
    for copy in second:
        copy.wait()
    d_slot_out = dot3(split(combine), split(cotangent_ref[...]), ((1,), (0,)))
    for k in range(4):
        sent_ref[k * e : (k + 1) * e, 0, :d] = slot_in
        sent_ref[k * e : (k + 1) * e, 0, d:] = d_slot_out


def route(tokens, cotangent, router_t):
    e, d = router_t.shape
    p = tokens.shape[0]
    f32 = jnp.float32
    return pl.pallas_call(
        route_kernel,
        out_shape=(
            jax.ShapeDtypeStruct((4 * e, 1, 2 * d), f32),
            jax.ShapeDtypeStruct((e, p), f32),
            jax.ShapeDtypeStruct((e, p), f32),
        ),
        in_specs=[
            pl.BlockSpec(memory_space=pltpu.HBM),
            pl.BlockSpec(memory_space=pltpu.HBM),
            pl.BlockSpec(memory_space=pltpu.VMEM),
        ],
        scratch_shapes=[
            pltpu.VMEM((p, d), f32),
            pltpu.VMEM((p, d), f32),
            pltpu.SemaphoreType.DMA((2, PIECES)),
        ],
        compiler_params=pltpu.CompilerParams(vmem_limit_bytes=56 * 2**20),
        name="route",
    )(tokens, cotangent, router_t)


def finish_kernel(
    back_hbm, tokens_ref, cotangent_ref, dispatch_ref, combine_ref, local_ref, weights_ref, slots_ref,
    back_ref, sems
):
    e, p = dispatch_ref.shape
    d = tokens_ref.shape[1]
    copies = fetch(back_hbm, back_ref, sems)
    for copy in copies:
        copy.start()
    total = None
    for k in range(4):
        copies[k].wait()
        rows = back_ref[k * e : (k + 1) * e, 0, :]
        total = rows if total is None else total + rows
    slot_out, d_slot_in = total[:, :d], total[:, d:]
    slots_ref[...] = d_slot_in
    dispatch, combine = dispatch_ref[...], combine_ref[...]
    tokens = split(tokens_ref[...])
    d_disp = dot3(split(d_slot_in), tokens, ((1,), (1,)))
    d_comb = dot3(split(slot_out), split(cotangent_ref[...]), ((1,), (1,)))
    d_logits = dispatch * (d_disp - jnp.sum(dispatch * d_disp, axis=1, keepdims=True))
    d_logits = d_logits + combine * (d_comb - jnp.sum(combine * d_comb, axis=0, keepdims=True))
    weights_ref[:e, :] = dispatch
    weights_ref[e:, :] = d_logits
    local_ref[...] = dot3(split(d_logits), tokens, ((1,), (0,)))


def finish(back, halves, dispatch, combine):
    e, p = dispatch.shape
    d = back.shape[2] // 2
    f32 = jnp.float32
    return pl.pallas_call(
        finish_kernel,
        out_shape=(
            jax.ShapeDtypeStruct((e, d), f32),
            jax.ShapeDtypeStruct((2 * e, p), f32),
            jax.ShapeDtypeStruct((e, d), f32),
        ),
        in_specs=[pl.BlockSpec(memory_space=pltpu.HBM)] + [pl.BlockSpec(memory_space=pltpu.VMEM)] * 4,
        scratch_shapes=[pltpu.VMEM(back.shape, f32), pltpu.SemaphoreType.DMA((PIECES,))],
        compiler_params=pltpu.CompilerParams(vmem_limit_bytes=24 * 2**20),
        name="finish",
    )(back, *halves, dispatch, combine)


def on_device(tokens, router, w_in, w_out, cotangent):
    tokens, cotangent = tokens[0], cotangent[0]
    w_in, w_out = w_in[0], w_out[0]
    width = tokens.shape[1]
    n_exp = router.shape[1]
    router_t = router.T
    sent, dispatch, combine = route(tokens, cotangent, router_t)
    arrived = lax.all_to_all(sent, ZEX, 0, 0, tiled=True).reshape(4 * n_exp, 2 * width)
    x = gather_y(arrived[:, :width])
    dy = gather_y(arrived[:, width:])
    pre_act = jnp.einsum("rd,dh->rh", x, w_in, precision=high)
    hidden, gelu_pull = jax.vjp(jax.nn.gelu, pre_act)
    d_hidden = jnp.einsum("rd,hd->rh", dy, w_out, precision=high)
    d_pre = gelu_pull(d_hidden)[0]
    part_out = jnp.einsum("rh,hd->rd", hidden, w_out, precision=high)
    part_grad = jnp.einsum("rh,dh->rd", d_pre, w_in, precision=high)
    summed = jnp.concatenate([scatter_y(part_out), scatter_y(part_grad)], axis=1)
    grad_w_out = jnp.einsum("rh,rd->hd", hidden, dy, precision=high)
    grad_w_in = jnp.einsum("rd,rh->dh", x, d_pre, precision=high)
    back = lax.all_to_all(summed.reshape(4 * n_exp, 1, 2 * width), ZEX, 0, 0, tiled=True)
    halves = tokens, cotangent
    back, grad_w_in, grad_w_out = lax.optimization_barrier((back, grad_w_in, grad_w_out))
    local_router, weights, d_slot_in = finish(back, halves, dispatch, combine)
    slots = jnp.concatenate([d_slot_in, router_t])
    grad_tokens = jnp.einsum("kp,kd->pd", weights, slots, precision=high)
    grad_router, grad_tokens = sum_all(local_router, grad_tokens)
    grad_router = grad_router.T
    return (grad_tokens[None], grad_router, grad_w_in[None], grad_w_out[None])


def solution(mesh):
    split = Mesh(mesh.devices.reshape(4, 4, 2, 4, 2), ALL)
    return jax.shard_map(
        on_device,
        mesh=split,
        in_specs=(
            P(ALL, None, None),
            P(),
            P(EX, None, DP),
            P(EX, DP, None),
            P(ALL, None, None),
        ),
        out_specs=(
            P(ALL, None, None),
            P(),
            P(EX, None, DP),
            P(EX, DP, None),
        ),
        check_vma=False,
    )
```

```python
import jax
import jax.numpy as jnp
from jax import lax
from jax.experimental import pallas as pl
from jax.experimental.pallas import tpu as pltpu
from jax.sharding import Mesh, PartitionSpec as P

highest = lax.Precision.HIGHEST
high = lax.Precision.HIGH

DP = ("zl", "y")
EX = ("zh", "x", "c")
ZEX = ("zl",) + EX
ALL = DP + EX
UP = [(i, (i + 1) % 4) for i in range(4)]
DOWN = [(i, (i - 1) % 4) for i in range(4)]


def gather_y(block):
    half = block.shape[0] // 2
    from_below = lax.ppermute(block, "y", UP)
    from_above = lax.ppermute(block, "y", DOWN)
    far_a = lax.ppermute(from_below[:half], "y", UP)
    far_b = lax.ppermute(from_above[half:], "y", DOWN)
    return jnp.concatenate([block, from_below, from_above, far_a, far_b])


def send_first(parts):
    n = parts.shape[0] // 4
    half = n // 2
    below, above, far = parts[n : 2 * n], parts[2 * n : 3 * n], parts[3 * n :]
    down = lax.ppermute(jnp.concatenate([below[half:], far[:half]]), "y", DOWN)
    up = lax.ppermute(jnp.concatenate([above[:half], far[half:]]), "y", UP)
    down, up = lax.optimization_barrier((down, up))
    return down, up, below[:half] + down[half:], above[half:] + up[half:]


def scatter_both(out, grad):
    down_o, up_o, low_o, top_o = send_first(out)
    down_g, up_g, low_g, top_g = send_first(grad)
    low, top = jnp.concatenate([low_o, low_g], axis=1), jnp.concatenate([top_o, top_g], axis=1)
    low, top = lax.optimization_barrier((low, top))
    low, top = lax.ppermute(low, "y", DOWN), lax.ppermute(top, "y", UP)
    low, top = lax.optimization_barrier((low, top))
    return join(out, grad, down_o, up_o, down_g, up_g, low, top)


def join_kernel(out, grad, down_o, up_o, down_g, up_g, low, top, joined):
    half, width = low.shape[0], out.shape[1]
    for k, (parts, down, up) in enumerate(((out, down_o, up_o), (grad, down_g, up_g))):
        columns = pl.ds(k * width, width)
        joined[:half, 0, columns] = parts[:half, :] + up[:half, :] + low[:, columns]
        joined[half:, 0, columns] = parts[half : 2 * half, :] + down[:half, :] + top[:, columns]


def join(*pieces):
    n, width = pieces[2].shape
    return pl.pallas_call(
        join_kernel,
        out_shape=jax.ShapeDtypeStruct((n, 1, 2 * width), jnp.float32),
        compiler_params=pltpu.CompilerParams(vmem_limit_bytes=24 * 2**20),
        name="join",
    )(*pieces)


def sum_axis(block, axis):
    total = block
    for k in range(1, 4):
        total = total + lax.ppermute(block, axis, [(i, (i + k) % 4) for i in range(4)])
    return total


def sum_all(local, beside):
    swap = [(0, 1), (1, 0)]
    first = lax.axis_index("c") == 0
    half = local.shape[0] // 2
    low, top = local[:half], local[half:]
    mine = jnp.where(first, low, top) + lax.ppermute(jnp.where(first, top, low), "c", swap)
    mine = sum_axis(sum_axis(mine, "x"), "y")
    pieces = jnp.broadcast_to(mine[None], (8,) + mine.shape)
    mine = jnp.sum(lax.all_to_all(pieces, ("zl", "zh"), 0, 0, tiled=True), axis=0)
    mine, beside = lax.optimization_barrier((mine, beside))
    other = lax.ppermute(mine, "c", swap)
    return jnp.where(first, jnp.concatenate([mine, other]), jnp.concatenate([other, mine])), beside


def split(a):
    top = a.astype(jnp.bfloat16)
    return top, (a - top.astype(jnp.float32)).astype(jnp.bfloat16)


def dot3(a, b, dims):
    (a_top, a_low), (b_top, b_low) = a, b
    dot = lambda u, v: lax.dot_general(u, v, (dims, ((), ())), preferred_element_type=jnp.float32)
    return dot(a_low, b_top) + dot(a_top, b_low) + dot(a_top, b_top)


PIECES = 4


def fetch(source, target, sems):
    rows = target.shape[0] // PIECES
    return [
        pltpu.make_async_copy(
            source.at[pl.ds(k * rows, rows)], target.at[pl.ds(k * rows, rows)], sems.at[k]
        )
        for k in range(PIECES)
    ]


def route_kernel(tokens_ref, cotangent_ref, router_ref, sent_ref, dispatch_ref, combine_ref):
    e, d = router_ref.shape
    tokens = tokens_ref[...]
    logits = lax.dot_general(
        router_ref[...], tokens, (((1,), (1,)), ((), ())), precision=highest, preferred_element_type=jnp.float32
    )
    by_token = jnp.exp(logits - jnp.max(logits, axis=1, keepdims=True))
    dispatch = by_token / jnp.sum(by_token, axis=1, keepdims=True)
    by_expert = jnp.exp(logits - jnp.max(logits, axis=0, keepdims=True))
    combine = by_expert / jnp.sum(by_expert, axis=0, keepdims=True)
    dispatch_ref[...] = dispatch
    combine_ref[...] = combine
    slot_in = dot3(split(dispatch), split(tokens), ((1,), (0,)))
    d_slot_out = dot3(split(combine), split(cotangent_ref[...]), ((1,), (0,)))
    for k in range(4):
        sent_ref[k * e : (k + 1) * e, 0, :d] = slot_in
        sent_ref[k * e : (k + 1) * e, 0, d:] = d_slot_out


def route(tokens, cotangent, router_t):
    e, d = router_t.shape
    p = tokens.shape[0]
    f32 = jnp.float32
    return pl.pallas_call(
        route_kernel,
        out_shape=(
            jax.ShapeDtypeStruct((4 * e, 1, 2 * d), f32),
            jax.ShapeDtypeStruct((e, p), f32),
            jax.ShapeDtypeStruct((e, p), f32),
        ),
        compiler_params=pltpu.CompilerParams(vmem_limit_bytes=24 * 2**20),
        name="route",
    )(tokens, cotangent, router_t)


def finish_kernel(
    back_hbm, tokens_ref, cotangent_ref, dispatch_ref, combine_ref, local_ref, weights_ref, slots_ref,
    back_ref, sems
):
    e, p = dispatch_ref.shape
    d = tokens_ref.shape[1]
    copies = fetch(back_hbm, back_ref, sems)
    for copy in copies:
        copy.start()
    total = None
    for k in range(4):
        copies[k].wait()
        rows = back_ref[k * e : (k + 1) * e, 0, :]
        total = rows if total is None else total + rows
    slot_out, d_slot_in = total[:, :d], total[:, d:]
    slots_ref[...] = d_slot_in
    dispatch, combine = dispatch_ref[...], combine_ref[...]
    tokens = split(tokens_ref[...])
    d_disp = dot3(split(d_slot_in), tokens, ((1,), (1,)))
    d_comb = dot3(split(slot_out), split(cotangent_ref[...]), ((1,), (1,)))
    d_logits = dispatch * (d_disp - jnp.sum(dispatch * d_disp, axis=1, keepdims=True))
    d_logits = d_logits + combine * (d_comb - jnp.sum(combine * d_comb, axis=0, keepdims=True))
    weights_ref[:e, :] = dispatch
    weights_ref[e:, :] = d_logits
    local_ref[...] = dot3(split(d_logits), tokens, ((1,), (0,)))


def finish(back, halves, dispatch, combine):
    e, p = dispatch.shape
    d = back.shape[2] // 2
    f32 = jnp.float32
    return pl.pallas_call(
        finish_kernel,
        out_shape=(
            jax.ShapeDtypeStruct((e, d), f32),
            jax.ShapeDtypeStruct((2 * e, p), f32),
            jax.ShapeDtypeStruct((e, d), f32),
        ),
        in_specs=[pl.BlockSpec(memory_space=pltpu.HBM)] + [pl.BlockSpec(memory_space=pltpu.VMEM)] * 4,
        scratch_shapes=[pltpu.VMEM(back.shape, f32), pltpu.SemaphoreType.DMA((PIECES,))],
        compiler_params=pltpu.CompilerParams(vmem_limit_bytes=24 * 2**20),
        name="finish",
    )(back, *halves, dispatch, combine)


def on_device(tokens, router, w_in, w_out, cotangent):
    tokens, cotangent = tokens[0], cotangent[0]
    w_in, w_out = w_in[0], w_out[0]
    width = tokens.shape[1]
    n_exp = router.shape[1]
    router_t = router.T
    sent, dispatch, combine = route(tokens, cotangent, router_t)
    arrived = lax.all_to_all(sent, ZEX, 0, 0, tiled=True).reshape(4 * n_exp, 2 * width)
    x = gather_y(arrived[:, :width])
    dy = gather_y(arrived[:, width:])
    pre_act = jnp.einsum("rd,dh->rh", x, w_in, precision=high)
    hidden, gelu_pull = jax.vjp(jax.nn.gelu, pre_act)
    d_hidden = jnp.einsum("rd,hd->rh", dy, w_out, precision=high)
    d_pre = gelu_pull(d_hidden)[0]
    part_out = jnp.einsum("rh,hd->rd", hidden, w_out, precision=high)
    part_grad = jnp.einsum("rh,dh->rd", d_pre, w_in, precision=high)
    summed = scatter_both(part_out, part_grad)
    grad_w_out = jnp.einsum("rh,rd->hd", hidden, dy, precision=high)
    grad_w_in = jnp.einsum("rd,rh->dh", x, d_pre, precision=high)
    back = lax.all_to_all(summed, ZEX, 0, 0, tiled=True)
    halves = tokens, cotangent
    back, grad_w_in, grad_w_out = lax.optimization_barrier((back, grad_w_in, grad_w_out))
    local_router, weights, d_slot_in = finish(back, halves, dispatch, combine)
    slots = jnp.concatenate([d_slot_in, router_t])
    grad_tokens = jnp.einsum("kp,kd->pd", weights, slots, precision=high)
    grad_router, grad_tokens = sum_all(local_router, grad_tokens)
    grad_router = grad_router.T
    return (grad_tokens[None], grad_router, grad_w_in[None], grad_w_out[None])


def solution(mesh):
    split = Mesh(mesh.devices.reshape(4, 4, 2, 4, 2), ALL)
    return jax.shard_map(
        on_device,
        mesh=split,
        in_specs=(
            P(ALL, None, None),
            P(),
            P(EX, None, DP),
            P(EX, DP, None),
            P(ALL, None, None),
        ),
        out_specs=(
            P(ALL, None, None),
            P(),
            P(EX, None, DP),
            P(EX, DP, None),
        ),
        check_vma=False,
    )
```

```python
import jax
import jax.numpy as jnp
from jax import lax
from jax.experimental import pallas as pl
from jax.experimental.pallas import tpu as pltpu
from jax.sharding import Mesh, PartitionSpec as P

highest = lax.Precision.HIGHEST
high = lax.Precision.HIGH

DP = ("zl", "y")
EX = ("zh", "x", "c")
ZEX = ("zl",) + EX
ALL = DP + EX
UP = [(i, (i + 1) % 4) for i in range(4)]
DOWN = [(i, (i - 1) % 4) for i in range(4)]


def gather_y(block):
    half = block.shape[0] // 2
    from_below = lax.ppermute(block, "y", UP)
    from_above = lax.ppermute(block, "y", DOWN)
    far_a = lax.ppermute(from_below[:half], "y", UP)
    far_b = lax.ppermute(from_above[half:], "y", DOWN)
    return jnp.concatenate([block, from_below, from_above, far_a, far_b])


def send_first(parts):
    n = parts.shape[0] // 4
    half = n // 2
    below, above, far = parts[n : 2 * n], parts[2 * n : 3 * n], parts[3 * n :]
    down = lax.ppermute(jnp.concatenate([below[half:], far[:half]]), "y", DOWN)
    up = lax.ppermute(jnp.concatenate([above[:half], far[half:]]), "y", UP)
    down, up = lax.optimization_barrier((down, up))
    return down, up, below[:half] + down[half:], above[half:] + up[half:]


def scatter_both(out, grad):
    down_o, up_o, low_o, top_o = send_first(out)
    down_g, up_g, low_g, top_g = send_first(grad)
    low, top = jnp.concatenate([low_o, low_g], axis=1), jnp.concatenate([top_o, top_g], axis=1)
    low, top = lax.optimization_barrier((low, top))
    low, top = lax.ppermute(low, "y", DOWN), lax.ppermute(top, "y", UP)
    low, top = lax.optimization_barrier((low, top))
    return join(out, grad, down_o, up_o, down_g, up_g, low, top)


def join_kernel(out, grad, down_o, up_o, down_g, up_g, low, top, joined):
    half, width = low.shape[0], out.shape[1]
    for k, (parts, down, up) in enumerate(((out, down_o, up_o), (grad, down_g, up_g))):
        columns = pl.ds(k * width, width)
        joined[:half, 0, columns] = parts[:half, :] + up[:half, :] + low[:, columns]
        joined[half:, 0, columns] = parts[half : 2 * half, :] + down[:half, :] + top[:, columns]


def join(*pieces):
    n, width = pieces[2].shape
    return pl.pallas_call(
        join_kernel,
        out_shape=jax.ShapeDtypeStruct((n, 1, 2 * width), jnp.float32),
        compiler_params=pltpu.CompilerParams(vmem_limit_bytes=24 * 2**20),
        name="join",
    )(*pieces)


def sum_axis(block, axis):
    total = block
    for k in (2, 1, 3):
        total = total + lax.ppermute(block, axis, [(i, (i + k) % 4) for i in range(4)])
    return total


def sum_all(local, beside):
    swap = [(0, 1), (1, 0)]
    first = lax.axis_index("c") == 0
    half = local.shape[0] // 2
    low, top = local[:half], local[half:]
    mine = jnp.where(first, low, top) + lax.ppermute(jnp.where(first, top, low), "c", swap)
    mine = sum_axis(sum_axis(mine, "x"), "y")
    pieces = jnp.broadcast_to(mine[None], (8,) + mine.shape)
    mine = jnp.sum(lax.all_to_all(pieces, ("zl", "zh"), 0, 0, tiled=True), axis=0)
    mine, beside = lax.optimization_barrier((mine, beside))
    other = lax.ppermute(mine, "c", swap)
    return jnp.where(first, jnp.concatenate([mine, other]), jnp.concatenate([other, mine])), beside


def split(a):
    top = a.astype(jnp.bfloat16)
    return top, (a - top.astype(jnp.float32)).astype(jnp.bfloat16)


def dot3(a, b, dims):
    (a_top, a_low), (b_top, b_low) = a, b
    dot = lambda u, v: lax.dot_general(u, v, (dims, ((), ())), preferred_element_type=jnp.float32)
    return dot(a_low, b_top) + dot(a_top, b_low) + dot(a_top, b_top)


PIECES = 4


def fetch(source, target, sems):
    rows = target.shape[0] // PIECES
    return [
        pltpu.make_async_copy(
            source.at[pl.ds(k * rows, rows)], target.at[pl.ds(k * rows, rows)], sems.at[k]
        )
        for k in range(PIECES)
    ]


def route_kernel(tokens_ref, cotangent_ref, router_ref, sent_ref, dispatch_ref, combine_ref):
    e, d = router_ref.shape
    tokens = tokens_ref[...]
    logits = lax.dot_general(
        router_ref[...], tokens, (((1,), (1,)), ((), ())), precision=highest, preferred_element_type=jnp.float32
    )
    by_token = jnp.exp(logits - jnp.max(logits, axis=1, keepdims=True))
    dispatch = by_token / jnp.sum(by_token, axis=1, keepdims=True)
    by_expert = jnp.exp(logits - jnp.max(logits, axis=0, keepdims=True))
    combine = by_expert / jnp.sum(by_expert, axis=0, keepdims=True)
    dispatch_ref[...] = dispatch
    combine_ref[...] = combine
    slot_in = dot3(split(dispatch), split(tokens), ((1,), (0,)))
    d_slot_out = dot3(split(combine), split(cotangent_ref[...]), ((1,), (0,)))
    for k in range(4):
        sent_ref[k * e : (k + 1) * e, 0, :d] = slot_in
        sent_ref[k * e : (k + 1) * e, 0, d:] = d_slot_out


def route(tokens, cotangent, router_t):
    e, d = router_t.shape
    p = tokens.shape[0]
    f32 = jnp.float32
    return pl.pallas_call(
        route_kernel,
        out_shape=(
            jax.ShapeDtypeStruct((4 * e, 1, 2 * d), f32),
            jax.ShapeDtypeStruct((e, p), f32),
            jax.ShapeDtypeStruct((e, p), f32),
        ),
        compiler_params=pltpu.CompilerParams(vmem_limit_bytes=24 * 2**20),
        name="route",
    )(tokens, cotangent, router_t)


def finish_kernel(
    back_hbm, tokens_ref, cotangent_ref, dispatch_ref, combine_ref, local_ref, weights_ref, slots_ref,
    back_ref, sems
):
    e, p = dispatch_ref.shape
    d = tokens_ref.shape[1]
    copies = fetch(back_hbm, back_ref, sems)
    for copy in copies:
        copy.start()
    total = None
    for k in range(4):
        copies[k].wait()
        rows = back_ref[k * e : (k + 1) * e, 0, :]
        total = rows if total is None else total + rows
    slot_out, d_slot_in = total[:, :d], total[:, d:]
    slots_ref[...] = d_slot_in
    dispatch, combine = dispatch_ref[...], combine_ref[...]
    tokens = split(tokens_ref[...])
    d_disp = dot3(split(d_slot_in), tokens, ((1,), (1,)))
    d_comb = dot3(split(slot_out), split(cotangent_ref[...]), ((1,), (1,)))
    d_logits = dispatch * (d_disp - jnp.sum(dispatch * d_disp, axis=1, keepdims=True))
    d_logits = d_logits + combine * (d_comb - jnp.sum(combine * d_comb, axis=0, keepdims=True))
    weights_ref[:e, :] = dispatch
    weights_ref[e:, :] = d_logits
    local_ref[...] = dot3(split(d_logits), tokens, ((1,), (0,)))


def finish(back, halves, dispatch, combine):
    e, p = dispatch.shape
    d = back.shape[2] // 2
    f32 = jnp.float32
    return pl.pallas_call(
        finish_kernel,
        out_shape=(
            jax.ShapeDtypeStruct((e, d), f32),
            jax.ShapeDtypeStruct((2 * e, p), f32),
            jax.ShapeDtypeStruct((e, d), f32),
        ),
        in_specs=[pl.BlockSpec(memory_space=pltpu.HBM)] + [pl.BlockSpec(memory_space=pltpu.VMEM)] * 4,
        scratch_shapes=[pltpu.VMEM(back.shape, f32), pltpu.SemaphoreType.DMA((PIECES,))],
        compiler_params=pltpu.CompilerParams(vmem_limit_bytes=24 * 2**20),
        name="finish",
    )(back, *halves, dispatch, combine)


def on_device(tokens, router, w_in, w_out, cotangent):
    tokens, cotangent = tokens[0], cotangent[0]
    w_in, w_out = w_in[0], w_out[0]
    width = tokens.shape[1]
    n_exp = router.shape[1]
    router_t = router.T
    sent, dispatch, combine = route(tokens, cotangent, router_t)
    arrived = lax.all_to_all(sent, ZEX, 0, 0, tiled=True).reshape(4 * n_exp, 2 * width)
    x = gather_y(arrived[:, :width])
    dy = gather_y(arrived[:, width:])
    pre_act = jnp.einsum("rd,dh->rh", x, w_in, precision=high)
    hidden, gelu_pull = jax.vjp(jax.nn.gelu, pre_act)
    d_hidden = jnp.einsum("rd,hd->rh", dy, w_out, precision=high)
    d_pre = gelu_pull(d_hidden)[0]
    part_out = jnp.einsum("rh,hd->rd", hidden, w_out, precision=high)
    part_grad = jnp.einsum("rh,dh->rd", d_pre, w_in, precision=high)
    summed = scatter_both(part_out, part_grad)
    grad_w_out = jnp.einsum("rh,rd->hd", hidden, dy, precision=high)
    grad_w_in = jnp.einsum("rd,rh->dh", x, d_pre, precision=high)
    back = lax.all_to_all(summed, ZEX, 0, 0, tiled=True)
    halves = tokens, cotangent
    back, grad_w_in, grad_w_out = lax.optimization_barrier((back, grad_w_in, grad_w_out))
    local_router, weights, d_slot_in = finish(back, halves, dispatch, combine)
    slots = jnp.concatenate([d_slot_in, router_t])
    grad_tokens = jnp.einsum("kp,kd->pd", weights, slots, precision=high)
    grad_router, grad_tokens = sum_all(local_router, grad_tokens)
    grad_router = grad_router.T
    return (grad_tokens[None], grad_router, grad_w_in[None], grad_w_out[None])


def solution(mesh):
    split = Mesh(mesh.devices.reshape(4, 4, 2, 4, 2), ALL)
    return jax.shard_map(
        on_device,
        mesh=split,
        in_specs=(
            P(ALL, None, None),
            P(),
            P(EX, None, DP),
            P(EX, DP, None),
            P(ALL, None, None),
        ),
        out_specs=(
            P(ALL, None, None),
            P(),
            P(EX, None, DP),
            P(EX, DP, None),
        ),
        check_vma=False,
    )
```

```python
import jax
import jax.numpy as jnp
from jax import lax
from jax.experimental import pallas as pl
from jax.experimental.pallas import tpu as pltpu
from jax.sharding import Mesh, PartitionSpec as P

highest = lax.Precision.HIGHEST
high = lax.Precision.HIGH

DP = ("zl", "y")
EX = ("zh", "x", "c")
ZEX = ("zl",) + EX
ALL = DP + EX
UP = [(i, (i + 1) % 4) for i in range(4)]
DOWN = [(i, (i - 1) % 4) for i in range(4)]


def gather_y(block):
    half = block.shape[0] // 2
    from_below = lax.ppermute(block, "y", UP)
    from_above = lax.ppermute(block, "y", DOWN)
    far_a = lax.ppermute(from_below[:half], "y", UP)
    far_b = lax.ppermute(from_above[half:], "y", DOWN)
    return jnp.concatenate([block, from_below, from_above, far_a, far_b])


def send_first(parts):
    n = parts.shape[0] // 4
    half = n // 2
    below, above, far = parts[n : 2 * n], parts[2 * n : 3 * n], parts[3 * n :]
    down = lax.ppermute(jnp.concatenate([below[half:], far[:half]]), "y", DOWN)
    up = lax.ppermute(jnp.concatenate([above[:half], far[half:]]), "y", UP)
    down, up = lax.optimization_barrier((down, up))
    return down, up, below[:half] + down[half:], above[half:] + up[half:]


def scatter_both(out, grad):
    down_o, up_o, low_o, top_o = send_first(out)
    down_g, up_g, low_g, top_g = send_first(grad)
    low, top = jnp.concatenate([low_o, low_g], axis=1), jnp.concatenate([top_o, top_g], axis=1)
    low, top = lax.optimization_barrier((low, top))
    low, top = lax.ppermute(low, "y", DOWN), lax.ppermute(top, "y", UP)
    low, top = lax.optimization_barrier((low, top))
    return join(out, grad, down_o, up_o, down_g, up_g, low, top)


def join_kernel(out, grad, down_o, up_o, down_g, up_g, low, top, joined):
    half, width = low.shape[0], out.shape[1]
    for k, (parts, down, up) in enumerate(((out, down_o, up_o), (grad, down_g, up_g))):
        columns = pl.ds(k * width, width)
        joined[:half, 0, columns] = parts[:half, :] + up[:half, :] + low[:, columns]
        joined[half:, 0, columns] = parts[half : 2 * half, :] + down[:half, :] + top[:, columns]


def join(*pieces):
    n, width = pieces[2].shape
    return pl.pallas_call(
        join_kernel,
        out_shape=jax.ShapeDtypeStruct((n, 1, 2 * width), jnp.float32),
        compiler_params=pltpu.CompilerParams(vmem_limit_bytes=24 * 2**20),
        name="join",
    )(*pieces)


def sum_axis(block, axis):
    total = block
    for k in (2, 1, 3):
        total = total + lax.ppermute(block, axis, [(i, (i + k) % 4) for i in range(4)])
    return total


def sum_all(local, beside):
    swap = [(0, 1), (1, 0)]
    first = lax.axis_index("c") == 0
    half = local.shape[0] // 2
    low, top = local[:half], local[half:]
    mine = jnp.where(first, low, top) + lax.ppermute(jnp.where(first, top, low), "c", swap)
    mine = sum_axis(sum_axis(mine, "y"), "x")
    pieces = jnp.broadcast_to(mine[None], (8,) + mine.shape)
    mine = jnp.sum(lax.all_to_all(pieces, ("zl", "zh"), 0, 0, tiled=True), axis=0)
    mine, beside = lax.optimization_barrier((mine, beside))
    other = lax.ppermute(mine, "c", swap)
    return jnp.where(first, jnp.concatenate([mine, other]), jnp.concatenate([other, mine])), beside


def split(a):
    top = a.astype(jnp.bfloat16)
    return top, (a - top.astype(jnp.float32)).astype(jnp.bfloat16)


def dot3(a, b, dims):
    (a_top, a_low), (b_top, b_low) = a, b
    dot = lambda u, v: lax.dot_general(u, v, (dims, ((), ())), preferred_element_type=jnp.float32)
    return dot(a_low, b_top) + dot(a_top, b_low) + dot(a_top, b_top)


PIECES = 4


def fetch(source, target, sems):
    rows = target.shape[0] // PIECES
    return [
        pltpu.make_async_copy(
            source.at[pl.ds(k * rows, rows)], target.at[pl.ds(k * rows, rows)], sems.at[k]
        )
        for k in range(PIECES)
    ]


def route_kernel(tokens_ref, cotangent_ref, router_ref, sent_ref, dispatch_ref, combine_ref):
    e, d = router_ref.shape
    tokens = tokens_ref[...]
    logits = lax.dot_general(
        router_ref[...], tokens, (((1,), (1,)), ((), ())), precision=highest, preferred_element_type=jnp.float32
    )
    by_token = jnp.exp(logits - jnp.max(logits, axis=1, keepdims=True))
    dispatch = by_token / jnp.sum(by_token, axis=1, keepdims=True)
    by_expert = jnp.exp(logits - jnp.max(logits, axis=0, keepdims=True))
    combine = by_expert / jnp.sum(by_expert, axis=0, keepdims=True)
    dispatch_ref[...] = dispatch
    combine_ref[...] = combine
    slot_in = dot3(split(dispatch), split(tokens), ((1,), (0,)))
    d_slot_out = dot3(split(combine), split(cotangent_ref[...]), ((1,), (0,)))
    for k in range(4):
        sent_ref[k * e : (k + 1) * e, 0, :d] = slot_in
        sent_ref[k * e : (k + 1) * e, 0, d:] = d_slot_out


def route(tokens, cotangent, router_t):
    e, d = router_t.shape
    p = tokens.shape[0]
    f32 = jnp.float32
    return pl.pallas_call(
        route_kernel,
        out_shape=(
            jax.ShapeDtypeStruct((4 * e, 1, 2 * d), f32),
            jax.ShapeDtypeStruct((e, p), f32),
            jax.ShapeDtypeStruct((e, p), f32),
        ),
        compiler_params=pltpu.CompilerParams(vmem_limit_bytes=24 * 2**20),
        name="route",
    )(tokens, cotangent, router_t)


def finish_kernel(
    back_hbm, tokens_ref, cotangent_ref, dispatch_ref, combine_ref, local_ref, weights_ref, slots_ref,
    back_ref, sems
):
    e, p = dispatch_ref.shape
    d = tokens_ref.shape[1]
    copies = fetch(back_hbm, back_ref, sems)
    for copy in copies:
        copy.start()
    total = None
    for k in range(4):
        copies[k].wait()
        rows = back_ref[k * e : (k + 1) * e, 0, :]
        total = rows if total is None else total + rows
    slot_out, d_slot_in = total[:, :d], total[:, d:]
    slots_ref[...] = d_slot_in
    dispatch, combine = dispatch_ref[...], combine_ref[...]
    tokens = split(tokens_ref[...])
    d_disp = dot3(split(d_slot_in), tokens, ((1,), (1,)))
    d_comb = dot3(split(slot_out), split(cotangent_ref[...]), ((1,), (1,)))
    d_logits = dispatch * (d_disp - jnp.sum(dispatch * d_disp, axis=1, keepdims=True))
    d_logits = d_logits + combine * (d_comb - jnp.sum(combine * d_comb, axis=0, keepdims=True))
    weights_ref[:e, :] = dispatch
    weights_ref[e:, :] = d_logits
    local_ref[...] = dot3(split(d_logits), tokens, ((1,), (0,)))


def finish(back, halves, dispatch, combine):
    e, p = dispatch.shape
    d = back.shape[2] // 2
    f32 = jnp.float32
    return pl.pallas_call(
        finish_kernel,
        out_shape=(
            jax.ShapeDtypeStruct((e, d), f32),
            jax.ShapeDtypeStruct((2 * e, p), f32),
            jax.ShapeDtypeStruct((e, d), f32),
        ),
        in_specs=[pl.BlockSpec(memory_space=pltpu.HBM)] + [pl.BlockSpec(memory_space=pltpu.VMEM)] * 4,
        scratch_shapes=[pltpu.VMEM(back.shape, f32), pltpu.SemaphoreType.DMA((PIECES,))],
        compiler_params=pltpu.CompilerParams(vmem_limit_bytes=24 * 2**20),
        name="finish",
    )(back, *halves, dispatch, combine)


def on_device(tokens, router, w_in, w_out, cotangent):
    tokens, cotangent = tokens[0], cotangent[0]
    w_in, w_out = w_in[0], w_out[0]
    width = tokens.shape[1]
    n_exp = router.shape[1]
    router_t = router.T
    sent, dispatch, combine = route(tokens, cotangent, router_t)
    arrived = lax.all_to_all(sent, ZEX, 0, 0, tiled=True).reshape(4 * n_exp, 2 * width)
    x = gather_y(arrived[:, :width])
    dy = gather_y(arrived[:, width:])
    pre_act = jnp.einsum("rd,dh->rh", x, w_in, precision=high)
    hidden, gelu_pull = jax.vjp(jax.nn.gelu, pre_act)
    d_hidden = jnp.einsum("rd,hd->rh", dy, w_out, precision=high)
    d_pre = gelu_pull(d_hidden)[0]
    part_out = jnp.einsum("rh,hd->rd", hidden, w_out, precision=high)
    part_grad = jnp.einsum("rh,dh->rd", d_pre, w_in, precision=high)
    summed = scatter_both(part_out, part_grad)
    grad_w_out = jnp.einsum("rh,rd->hd", hidden, dy, precision=high)
    grad_w_in = jnp.einsum("rd,rh->dh", x, d_pre, precision=high)
    back = lax.all_to_all(summed, ZEX, 0, 0, tiled=True)
    halves = tokens, cotangent
    back, grad_w_in, grad_w_out = lax.optimization_barrier((back, grad_w_in, grad_w_out))
    local_router, weights, d_slot_in = finish(back, halves, dispatch, combine)
    slots = jnp.concatenate([d_slot_in, router_t])
    grad_tokens = jnp.einsum("kp,kd->pd", weights, slots, precision=high)
    grad_router, grad_tokens = sum_all(local_router, grad_tokens)
    grad_router = grad_router.T
    return (grad_tokens[None], grad_router, grad_w_in[None], grad_w_out[None])


def solution(mesh):
    split = Mesh(mesh.devices.reshape(4, 4, 2, 4, 2), ALL)
    return jax.shard_map(
        on_device,
        mesh=split,
        in_specs=(
            P(ALL, None, None),
            P(),
            P(EX, None, DP),
            P(EX, DP, None),
            P(ALL, None, None),
        ),
        out_specs=(
            P(ALL, None, None),
            P(),
            P(EX, None, DP),
            P(EX, DP, None),
        ),
        check_vma=False,
    )
```
